256 devices in a mesh: lat: 16 (over z_lo, x, core), ord: 16 (over z_hi, y).
Axes of the slice: x: 4, y: 4, z: 8 (z_hi: 4, z_lo: 2; z = z_hi * 2 + z_lo), core: 2. Of those that a mesh axis runs over, the one named last changes fastest.
Arguments:
- altitude_grids: bfloat16 [2, 3072, 21600], P(None, 'lat', 'ord'), may hold values from -6 to 6
- polynomial_values: bfloat16 [32, 3072, 10802], P('ord', 'lat'), may hold values from -6 to 6
- span_azimuthal_modes: int32 [64], replicated, may hold values from 0 to 10800, as said below
- slot_mapping: int32 [64], replicated, may hold values from 0 to 63, as said below
Outputs:
- steepness: bfloat16 [2, 3072, 21600], P(None, 'lat', 'ord')
- curvature: bfloat16 [2, 3072, 21600], P(None, 'lat', 'ord')
The draws below stay inside these ranges and needn't reach their ends.
Inputs may be any that keep to these rules, and one draw needn't show every extreme that they name: `span_azimuthal_modes`: rising and distinct; the first 32 entries lie below 5400 and the first is 0; entry 63-i is 10800 minus entry i. `slot_mapping`: A permutation; slot 2k holds an entry below 32 and slot 2k+1 holds 63 minus it, so slots 2k and 2k+1 take orders m and 10800-m. Slot s lies on index s // 4 of ord.
All inputs are finite; a program needn't handle non-finite values.
Results may differ from the reference program's by a relative error of at most 0.0079.
Values sent between devices are 32-bit elements; how exact they have to be, the bound alone decides.
No kernel may reach another device: no remote copies, remote signals or barrier semaphores. Data moves between devices by JAX's collectives and lax.ppermute only.
A program may use at most 64 MiB of HBM per device.

```python
import math
import jax
import jax.numpy as jnp
from jax import lax

LMAX = 10800
MERIDIAN_AMOUNT = 21600
BAND = 64
ALTITUDE_SHEETS = 2
CYCLE_DEV = 192
NLAT = 10801
PACK = 10802
PERIOD_AMOUNT = 3072
N_LAT = 16


def draw_span_azimuthal_modes(key, part):
    key = jax.random.fold_in(key, 11)
    pool = jax.random.permutation(key, LMAX // 2 - 1) + 1
    lower = jnp.sort(pool[:BAND // 2 - 1])
    lower = jnp.concatenate([jnp.zeros((1,), jnp.int32), lower.astype(jnp.int32)])
    upper = (LMAX - lower)[::-1]
    return jnp.concatenate([lower, upper]).astype(jnp.int32)


def draw_slot_mapping(key, part):
    key = jax.random.fold_in(key, 23)
    picked = jax.random.permutation(key, BAND // 2).astype(jnp.int32)
    partner = BAND - 1 - picked
    return jnp.stack([picked, partner], axis=1).reshape(BAND).astype(jnp.int32)


def levels(stream_key, shape, split, least, largest):
    loudness = 1.0
    for dim, parts in split:
        draws = jax.random.uniform(jax.random.fold_in(jax.random.fold_in(stream_key, 6), dim), (parts,), jnp.float32, least / len(split), largest / len(split))
        loudness = loudness * jnp.repeat(jnp.exp(draws), shape[dim] // parts).reshape((-1,) + (1,) * (len(shape) - 1 - dim))
    return loudness


def scatter_about(key, shape, scale, limit, cuts=(), held_as=jnp.bfloat16):
    result = jax.random.normal(key, shape, jnp.float32) * scale
    if len(cuts) > 0:
        result = levels(key, shape, cuts, -0.22, 0.18) * result
    return jnp.clip(result, min=-limit, max=limit).astype(held_as)


def setup_inputs(seed: int = 0) -> dict:
    key_list = jax.random.split(jax.random.key(seed), 5)
    altitude_grids = scatter_about(key_list[0], (ALTITUDE_SHEETS, PERIOD_AMOUNT, MERIDIAN_AMOUNT), 1.0, 6.0, ((1, 16), (2, 16)))
    polynomial_values = scatter_about(key_list[1], (BAND // 2, PERIOD_AMOUNT, PACK), 1.0, 6.0, ((0, 16), (1, 16)))
    span_azimuthal_modes = draw_span_azimuthal_modes(jax.random.fold_in(key_list[4], 71), 0)
    slot_mapping = draw_slot_mapping(jax.random.fold_in(key_list[4], 71), 0)
    return dict(altitude_grids=altitude_grids, polynomial_values=polynomial_values, span_azimuthal_modes=span_azimuthal_modes, slot_mapping=slot_mapping)


def slot_orders(span_azimuthal_modes, slot_mapping):
    match = slot_mapping[:, None] == jnp.arange(BAND, dtype=jnp.int32)[None, :]
    return lax.optimization_barrier(jnp.sum(jnp.where(match, span_azimuthal_modes[None, :], 0), axis=1)).astype(jnp.int32)

def phases(orders, longitude):
    turns = orders[:, None] * longitude[None, :] % MERIDIAN_AMOUNT
    return turns.astype(jnp.float32) * (2.0 * math.pi / MERIDIAN_AMOUNT)

def colatitude(cycles, nring):
    return math.pi * (cycles.astype(jnp.float32) + 0.5 * (NLAT - nring + 1)) / NLAT

def variants(coeffs, first_order):
    pack = coeffs.shape[-1]
    position = jnp.arange(pack, dtype=jnp.int32)[None, :]
    first_len = (LMAX + 1 - first_order)[:, None]
    in_upper = position >= first_len
    degree = jnp.where(in_upper, position - 1, first_order[:, None] + position).astype(jnp.float32)
    order_val = jnp.where(in_upper, LMAX - first_order[:, None], first_order[:, None]).astype(jnp.float32)
    length = jnp.where(in_upper, first_order[:, None] + 1, first_len).astype(jnp.float32)
    scaling = 1.0 / jnp.sqrt(length)
    shifted = jnp.concatenate([coeffs[..., 1:], jnp.zeros_like(coeffs[..., :1])], axis=-1)
    shifted = jnp.where((position == first_len - 1)[:, None, None, :], 0.0, shifted)

    def spread(values):
        return values[:, None, None, :]
    stacked = jnp.stack([coeffs * spread(scaling), coeffs * spread(degree * scaling / LMAX), shifted * spread((degree + 1.0 + order_val) * scaling / LMAX), coeffs * spread(degree * (degree + 1.0) * scaling / (LMAX * LMAX))], axis=1)
    upper_mask = in_upper[:, None, None, None, :]
    return jnp.stack([jnp.where(upper_mask, 0.0, stacked), jnp.where(upper_mask, stacked, 0.0)], axis=1).astype(jnp.bfloat16)

def syntheses(synth, cycle_sine, cycle_cosine):
    slope_part = (cycle_cosine * synth[:, 1] - synth[:, 2]) / cycle_sine
    return jnp.stack([synth[:, 0], slope_part, synth[:, 3]], axis=1)

def derive(spectra, order_frac, cycle_sine):
    first = spectra[:, 0]
    slope_part = spectra[:, 1]
    laplace = spectra[:, 2]
    factor = order_frac[:, None, None] / cycle_sine
    square = factor * factor
    phi_grad = jnp.stack([-factor * first[:, 1], factor * first[:, 0]], axis=1)
    theta_theta = square[:, None] * first - laplace
    theta_phi = jnp.stack([-factor * slope_part[:, 1], factor * slope_part[:, 0]], axis=1)
    phi_phi = -square[:, None] * first
    return jnp.stack([slope_part, phi_grad, theta_theta, theta_phi, phi_phi], axis=1)

def surface(grid_fields):
    theta_grad = grid_fields[0]
    phi_grad = grid_fields[1]
    theta_theta = grid_fields[2]
    theta_phi = grid_fields[3]
    phi_phi = grid_fields[4]
    area = 1.0 + theta_grad * theta_grad + phi_grad * phi_grad
    steepness = jnp.sqrt(area)
    bending = ((1.0 + phi_grad * phi_grad) * theta_theta - 2.0 * theta_grad * phi_grad * theta_phi + (1.0 + theta_grad * theta_grad) * phi_phi) / (2.0 * area * steepness)
    return (steepness.astype(jnp.bfloat16), bending.astype(jnp.bfloat16))

def reference(altitude_grids, polynomial_values, span_azimuthal_modes, slot_mapping):
    orders = slot_orders(span_azimuthal_modes, slot_mapping)
    longitude = jnp.arange(MERIDIAN_AMOUNT, dtype=jnp.int32)
    cycles = jnp.arange(PERIOD_AMOUNT, dtype=jnp.int32)
    colat = colatitude(cycles, PERIOD_AMOUNT)
    cycle_sine = jnp.sin(colat)
    cycle_cosine = jnp.cos(colat)
    angles = phases(orders, longitude)
    forward_transform = (jnp.stack([jnp.cos(angles), -jnp.sin(angles)], axis=1) / math.sqrt(MERIDIAN_AMOUNT)).astype(jnp.bfloat16)
    forward_transform = forward_transform.reshape(2 * BAND, MERIDIAN_AMOUNT)
    altitude_lines = altitude_grids.reshape(ALTITUDE_SHEETS * PERIOD_AMOUNT, MERIDIAN_AMOUNT)
    cycle_coefficient = jnp.dot(altitude_lines, forward_transform.T, preferred_element_type=jnp.float32)
    cycle_coefficient = cycle_coefficient.reshape(ALTITUDE_SHEETS, PERIOD_AMOUNT, BAND, 2).transpose(2, 3, 0, 1)
    weighted = (cycle_coefficient * cycle_sine / math.sqrt(PERIOD_AMOUNT)).astype(jnp.bfloat16)
    weighted = weighted.reshape(BAND // 2, 2, 2, ALTITUDE_SHEETS, PERIOD_AMOUNT)
    first_order = orders.reshape(BAND // 2, 2)[:, 0]
    position = jnp.arange(PACK, dtype=jnp.int32)

    def one_pair(items):
        table, rows, start_order = items
        product = jnp.dot(rows.reshape(4 * ALTITUDE_SHEETS, PERIOD_AMOUNT), table, preferred_element_type=jnp.float32)
        product = product.reshape(2, 2, ALTITUDE_SHEETS, PACK)
        in_upper = position >= LMAX + 1 - start_order
        coeffs = jnp.where(in_upper, product[1], product[0])
        weights = variants(coeffs[None], start_order[None])[0]
        synth = jnp.dot(weights.reshape(16 * ALTITUDE_SHEETS, PACK), table.T, preferred_element_type=jnp.float32)
        return synth.reshape(2, 4, 2, ALTITUDE_SHEETS, PERIOD_AMOUNT)
    synth = lax.map(one_pair, (polynomial_values, weighted, first_order)).reshape(BAND, 4, 2, ALTITUDE_SHEETS, PERIOD_AMOUNT)
    spectra = syntheses(synth, cycle_sine, cycle_cosine)
    order_frac = orders.astype(jnp.float32) / LMAX
    spectral = derive(spectra, order_frac, cycle_sine)
    inv_table = jnp.stack([jnp.cos(angles), -jnp.sin(angles)], axis=1) / math.sqrt(BAND)

    def one_band(index):
        block = lax.dynamic_slice_in_dim(spectral, (index * CYCLE_DEV).astype(jnp.int32), CYCLE_DEV, axis=4)
        grid_fields = jnp.einsum('scxfr,sxj->cfrj', block, inv_table, precision=lax.Precision.HIGHEST)
        return surface(grid_fields)
    steep_blocks, bend_blocks = lax.map(one_band, jnp.arange(N_LAT, dtype=jnp.int32))
    steepness = steep_blocks.transpose(1, 0, 2, 3).reshape(ALTITUDE_SHEETS, PERIOD_AMOUNT, MERIDIAN_AMOUNT)
    curvature = bend_blocks.transpose(1, 0, 2, 3).reshape(ALTITUDE_SHEETS, PERIOD_AMOUNT, MERIDIAN_AMOUNT)
    return (steepness, curvature)
```

```python
import math

import jax
import jax.numpy as jnp
from jax import lax
from jax.sharding import PartitionSpec as P

LMAX = 10800
MERIDIAN_AMOUNT = 21600
BAND = 64
NLAT = 10801


def slot_orders(span_azimuthal_modes, slot_mapping):
    match = slot_mapping[:, None] == jnp.arange(BAND, dtype=jnp.int32)[None, :]
    return jnp.sum(jnp.where(match, span_azimuthal_modes[None, :], 0), axis=1)


def phases(orders, longitude):
    turns = orders[:, None] * longitude[None, :] % MERIDIAN_AMOUNT
    return turns.astype(jnp.float32) * (2.0 * math.pi / MERIDIAN_AMOUNT)


def colatitude(cycles, nring):
    return math.pi * (cycles.astype(jnp.float32) + 0.5 * (NLAT - nring + 1)) / NLAT


def variants(coeffs, first_order):
    pack = coeffs.shape[-1]
    position = jnp.arange(pack, dtype=jnp.int32)
    first_len = LMAX + 1 - first_order
    in_upper = position >= first_len
    degree = jnp.where(in_upper, position - 1, first_order + position).astype(jnp.float32)
    order_val = jnp.where(in_upper, LMAX - first_order, first_order).astype(jnp.float32)
    length = jnp.where(in_upper, first_order + 1, first_len).astype(jnp.float32)
    scaling = 1.0 / jnp.sqrt(length)
    shifted = jnp.concatenate([coeffs[..., 1:], jnp.zeros_like(coeffs[..., :1])], axis=-1)
    shifted = jnp.where(position == first_len - 1, 0.0, shifted)
    stacked = jnp.stack(
        [
            coeffs * scaling,
            coeffs * (degree * scaling / LMAX),
            shifted * ((degree + 1.0 + order_val) * scaling / LMAX),
            coeffs * (degree * (degree + 1.0) * scaling / (LMAX * LMAX)),
        ]
    )
    return jnp.stack(
        [jnp.where(in_upper, 0.0, stacked), jnp.where(in_upper, stacked, 0.0)]
    ).astype(jnp.bfloat16)


def surface(p, q, r, s, t):
    area = 1.0 + p * p + q * q
    steepness = jnp.sqrt(area)
    bending = ((1.0 + q * q) * r - 2.0 * p * q * s + (1.0 + p * p) * t) / (2.0 * area * steepness)
    return steepness.astype(jnp.bfloat16), bending.astype(jnp.bfloat16)


def swap(value, axis, mask):
    return lax.ppermute(value, axis, [(k, k ^ mask) for k in range(lax.axis_size(axis))])


def on_device(altitude_grids, polynomial_values, span_azimuthal_modes, slot_mapping):
    layers, rings, meridians = altitude_grids.shape
    pack = polynomial_values.shape[2]
    n_ord = lax.axis_size("ord")
    nring = rings * lax.axis_size("lat")
    orders = slot_orders(span_azimuthal_modes, slot_mapping)
    longitude = lax.axis_index("ord") * meridians + jnp.arange(meridians, dtype=jnp.int32)
    cycles = lax.axis_index("lat") * rings + jnp.arange(rings, dtype=jnp.int32)
    colat = colatitude(cycles, nring)
    sine = jnp.sin(colat)
    cosine = jnp.cos(colat)
    angles = phases(orders, longitude)
    wave = jnp.stack([jnp.cos(angles), -jnp.sin(angles)], axis=1).reshape(2 * BAND, meridians)
    product = lax.dot_general(
        (wave / math.sqrt(MERIDIAN_AMOUNT)).astype(jnp.bfloat16),
        altitude_grids.reshape(layers * rings, meridians),
        (((1,), (1,)), ((), ())),
        preferred_element_type=jnp.float32,
    )
    parts = lax.all_to_all(
        product.reshape(n_ord, 8, layers * rings), "ord", 0, 0, tiled=True
    )
    cycle_coefficient = jnp.sum(parts, axis=0).reshape(2, 2, 2, layers, rings)
    weighted = (cycle_coefficient * sine / math.sqrt(nring)).astype(jnp.bfloat16)

    core = lax.axis_index("lat") % 2
    local_orders = lax.dynamic_slice_in_dim(orders, lax.axis_index("ord") * 4, 4)

    def analysis(pair):
        rows = lax.dynamic_index_in_dim(weighted, pair, 0, False)
        table = lax.dynamic_index_in_dim(polynomial_values, pair, 0, False)
        first_order = lax.dynamic_index_in_dim(local_orders, 2 * pair, 0, False)
        product = jnp.einsum("uxfr,rk->uxfk", rows, table, preferred_element_type=jnp.float32)
        in_upper = jnp.arange(pack, dtype=jnp.int32) >= LMAX + 1 - first_order
        return jnp.where(in_upper, product[1], product[0]).reshape(4, pack)

    coeffs = analysis(core) + swap(analysis(1 - core), "lat", 1)
    for mask in (2, 6, 8):
        coeffs = coeffs + swap(coeffs, "lat", mask)
    both = [coeffs, swap(coeffs, "lat", 1)]

    def synthesis(pair, coeffs):
        table = lax.dynamic_index_in_dim(polynomial_values, pair, 0, False)
        first_order = lax.dynamic_index_in_dim(local_orders, 2 * pair, 0, False)
        weights = variants(coeffs.reshape(2, layers, pack), first_order)
        synth = jnp.einsum("rk,ujxfk->juxfr", table, weights, preferred_element_type=jnp.float32)
        return jnp.stack([synth[0], (cosine * synth[1] - synth[2]) / sine, synth[3]])

    fields = jnp.stack([synthesis(core, both[0]), synthesis(1 - core, both[1])], axis=1)
    fields = fields.reshape(24, layers * rings)
    everything = lax.all_to_all(
        jnp.broadcast_to(fields[None], (n_ord,) + fields.shape), "ord", 0, 0, tiled=True
    ).reshape(n_ord, 3, 8, layers, rings)
    spectra = [everything[:, i].reshape(2 * BAND, layers, rings) for i in range(3)]

    def in_order(rows):
        split = rows.reshape(n_ord, 2, 4, -1)
        return jnp.where(core == 1, split[:, ::-1], split).reshape(rows.shape)

    fraction = in_order(jnp.repeat(orders.astype(jnp.float32) / LMAX, 2)[:, None])
    wave = in_order(wave) / math.sqrt(BAND)
    turned = wave.reshape(BAND, 2, meridians)
    turned = jnp.stack([turned[:, 1], -turned[:, 0]], axis=1).reshape(2 * BAND, meridians)

    def to_grid(rows, table):
        return jnp.einsum("kfr,kj->frj", rows, table, precision=lax.Precision.HIGH)

    first, slope, laplace = spectra
    p = to_grid(slope, wave)
    q = to_grid(first / sine, fraction * turned)
    t = -to_grid(first / (sine * sine), fraction * fraction * wave)
    r = -t - to_grid(laplace, wave)
    s = to_grid(slope / sine, fraction * turned)
    return surface(p, q, r, s, t)


def solution(mesh):
    return jax.shard_map(
        on_device,
        mesh=mesh,
        in_specs=(P(None, "lat", "ord"), P("ord", "lat", None), P(), P()),
        out_specs=(P(None, "lat", "ord"), P(None, "lat", "ord")),
        check_vma=False,
    )
```

```python
import functools
import math

import jax
import jax.numpy as jnp
from jax import lax
from jax.experimental import pallas as pl
from jax.experimental.pallas import tpu as pltpu
from jax.sharding import PartitionSpec as P

LMAX = 10800
MERIDIAN_AMOUNT = 21600
BAND = 64
NLAT = 10801
PACK = 10802
PADDED = 10880
WHOLE = 10752
RINGS = 192
MERIDIANS = 1350
ROWS = 2 * BAND

SINE_SERIES = tuple(
    (-1.0) ** n * (2.0 * math.pi) ** (2 * n + 1) / math.factorial(2 * n + 1) for n in range(8)
)


def swap(value, axis, mask):
    return lax.ppermute(value, axis, [(k, k ^ mask) for k in range(lax.axis_size(axis))])


def row_orders(modes, mapping, slot):
    lane = lax.broadcasted_iota(jnp.int32, (slot.shape[0], BAND), 1)
    entry = jnp.sum(
        jnp.where(lane == slot, mapping.astype(jnp.float32), 0.0), axis=1, keepdims=True
    ).astype(jnp.int32)
    return jnp.sum(
        jnp.where(lane == entry, modes.astype(jnp.float32), 0.0), axis=1, keepdims=True
    ).astype(jnp.int32)


def sine_turns(v):
    square = v * v
    total = SINE_SERIES[-1]
    for coefficient in SINE_SERIES[-2::-1]:
        total = total * square + coefficient
    return v * total


def cosine_of(orders, quarter, first):
    longitude = first + lax.broadcasted_iota(jnp.int32, (1, MERIDIANS), 1)
    product = orders * longitude
    cycles = (product.astype(jnp.float32) * (1.0 / MERIDIAN_AMOUNT)).astype(jnp.int32)
    turns = (product - cycles * MERIDIAN_AMOUNT + quarter * (MERIDIAN_AMOUNT // 4)).astype(
        jnp.float32
    ) * (1.0 / MERIDIAN_AMOUNT)
    turns = turns - jnp.round(turns)
    return sine_turns(0.25 - jnp.abs(turns))


def prepare_kernel(
    modes_ref,
    mapping_ref,
    table_ref,
    wave_ref,
    info_ref,
    orders_ref,
    held_ref,
    small_ref,
    sems,
    table_sems,
):
    copies = [
        pltpu.make_async_copy(modes_ref, small_ref.at[0], sems.at[0]),
        pltpu.make_async_copy(mapping_ref, small_ref.at[1], sems.at[1]),
    ]
    for copy in copies:
        copy.start()
    table_copies = []
    for pair in range(2):
        for block in range(4):
            rows = pl.ds(block * (RINGS // 4), RINGS // 4)
            copy = pltpu.make_async_copy(
                table_ref.at[pair, rows, :], held_ref.at[pair, rows, :], table_sems.at[pair * 4 + block]
            )
            copy.start()
            table_copies.append(copy)
    ord_index, lat_index = lax.axis_index("ord"), lax.axis_index("lat")
    core = lat_index % 2
    copies[0].wait()
    copies[1].wait()
    modes, mapping = small_ref[0], small_ref[1]
    row = lax.broadcasted_iota(jnp.int32, (ROWS, 1), 0)
    wave = cosine_of(row_orders(modes, mapping, row // 2), row % 2, ord_index * MERIDIANS)
    wave_ref[...] = (wave * (1.0 / math.sqrt(MERIDIAN_AMOUNT))).astype(jnp.bfloat16)

    row = lax.broadcasted_iota(jnp.int32, (8, 1), 0)
    slot = ord_index * 4 + (core + row) % 2 * 2
    first_orders = row_orders(modes, mapping, slot).astype(jnp.float32)
    lane = lax.broadcasted_iota(jnp.int32, (8, 2 * RINGS), 1)
    cycle = lat_index * RINGS + jnp.where(lane >= RINGS, lane - RINGS, lane)
    v = ((NLAT - 16 * RINGS * 1.0 + 1.0) * -0.5 + 0.5 * NLAT - cycle.astype(jnp.float32)) * (0.5 / NLAT)
    sine, cosine = sine_turns(0.25 - jnp.abs(v)), sine_turns(v)
    info_ref[...] = jnp.where(row == 0, sine, jnp.where(row == 1, cosine, first_orders))

    row = lax.broadcasted_iota(jnp.int32, (ROWS, 1), 0)
    slot = (row // 8) * 4 + ((row // 4) % 2 + core) % 2 * 2 + (row // 2) % 2
    orders_ref[...] = jnp.broadcast_to(row_orders(modes, mapping, slot), (ROWS, 128))

    for copy in table_copies:
        copy.wait()


def forward_kernel(wave_ref, grids_ref, out_ref):
    lines = grids_ref[...].reshape(2 * RINGS, MERIDIANS)
    out_ref[...] = lax.dot_general(
        wave_ref[...], lines, (((1,), (1,)), ((), ())), preferred_element_type=jnp.float32
    )


def table_kernel(orders_ref, after_ref, out_ref):
    row = lax.broadcasted_iota(jnp.int32, (ROWS, 1), 0)
    first = lax.axis_index("ord") * MERIDIANS
    orders = orders_ref[:, 0:1]
    fraction = orders.astype(jnp.float32) * (1.0 / LMAX)
    wave = cosine_of(orders, row % 2, first) * (1.0 / math.sqrt(BAND))
    turned = cosine_of(orders, row % 2 + 1, first) * (1.0 / math.sqrt(BAND))
    for index, table in enumerate((wave, fraction * turned, fraction * fraction * wave)):
        high = table.astype(jnp.bfloat16)
        low = (table - high.astype(jnp.float32)).astype(jnp.bfloat16)
        out_ref[index, 0:ROWS, :] = high
        out_ref[index, ROWS : 2 * ROWS, :] = high
        out_ref[index, 2 * ROWS :, :] = low


def analysis_kernel(which, parts_ref, info_ref, table_ref, out_ref):
    pair = (lax.axis_index("lat") + which) % 2
    first_len = LMAX + 1 - info_ref[2 + which : 3 + which, 0:1].astype(jnp.int32)
    total = parts_ref[0]
    for index in range(1, parts_ref.shape[0]):
        total = total + parts_ref[index]
    weighted = total * (info_ref[0:1, :] * (1.0 / math.sqrt(16 * RINGS)))
    mine = jnp.where(pair == 1, weighted[4:8], weighted[0:4])
    left, right = mine[:, :RINGS], mine[:, RINGS:]
    rows = jnp.concatenate([left[0:2], right[0:2], left[2:4], right[2:4]], axis=0).astype(
        jnp.bfloat16
    )
    step = 1536
    for start in range(0, PACK, step):
        size = min(step, PACK - start)
        product = jnp.dot(
            rows, table_ref[pair, :, start : start + size], preferred_element_type=jnp.float32
        )
        position = start + lax.broadcasted_iota(jnp.int32, (4, size), 1)
        out_ref[:, start : start + size] = jnp.where(
            position >= first_len, product[4:8], product[0:4]
        )
    out_ref[:, PACK:] = jnp.zeros((4, PADDED - PACK), jnp.float32)


def add_kernel(first_ref, second_ref, third_ref, fourth_ref, _, out_ref):
    out_ref[...] = (first_ref[...] + second_ref[...]) + (third_ref[...] + fourth_ref[...])


def synthesis_kernel(which, coeffs_ref, info_ref, table_ref, *rest):
    pair = (lax.axis_index("lat") + which) % 2
    order = info_ref[2 + which : 3 + which, 0:1].astype(jnp.int32)
    row = lax.broadcasted_iota(jnp.int32, (8, 1), 0)
    upper = (row // 2) % 2 == 1
    first_len = LMAX + 1 - order
    base = jnp.where(upper, -1, order)
    own_order = jnp.where(upper, LMAX - order, order)
    length = jnp.where(upper, order + 1, first_len).astype(jnp.float32)
    begin = jnp.where(upper, first_len, 0)
    end = jnp.where(upper, PACK, first_len)
    scaling = 1.0 / jnp.sqrt(length)
    step = 1536
    synth = jnp.zeros((32, RINGS), jnp.float32)
    for start in range(0, PADDED, step):
        size = min(step, PADDED - start)
        own = coeffs_ref[:, start : start + size]
        if start + size < PADDED:
            ahead = coeffs_ref[:, start + size : start + size + 128]
        else:
            ahead = jnp.zeros((4, 128), jnp.float32)
        wide = jnp.concatenate([own, ahead], axis=1)
        after = pltpu.roll(wide, size + 127, axis=1)[:, :size]
        spread = [jnp.concatenate([a[0:2], a[0:2], a[2:4], a[2:4]], axis=0) for a in (own, after)]
        position = start + lax.broadcasted_iota(jnp.int32, (8, size), 1)
        inside = (position >= begin) & (position < end)
        degree = (base + position).astype(jnp.float32)
        plain = jnp.where(inside, scaling, 0.0)
        sloped = plain * (degree * (1.0 / LMAX))
        ahead_factor = jnp.where(
            inside & (position < end - 1),
            (degree + (1.0 + own_order.astype(jnp.float32))) * (scaling * (1.0 / LMAX)),
            0.0,
        )
        curved = sloped * ((degree + 1.0) * (1.0 / LMAX))
        weights = jnp.concatenate(
            [spread[0] * plain, spread[0] * sloped, spread[1] * ahead_factor, spread[0] * curved],
            axis=0,
        ).astype(jnp.bfloat16)
        held = min(size, PACK - start)
        synth = synth + lax.dot_general(
            weights[:, :held],
            table_ref[pair, :, start : start + held],
            (((1,), (1,)), ((), ())),
            preferred_element_type=jnp.float32,
        )
    sine, cosine = info_ref[0:1, :RINGS], info_ref[1:2, :RINGS]
    fields = [synth[0:8], (cosine * synth[8:16] - synth[16:24]) / sine, synth[24:32]]
    fields = [jnp.concatenate([a[0:4], a[4:8]], axis=1) for a in fields]
    if which == 0:
        (out_ref,) = rest
        for index in range(3):
            out_ref[4 * index : 4 * index + 4, :] = fields[index]
    else:
        other_ref, _, out_ref = rest
        for index in range(3):
            rows = jnp.concatenate([other_ref[4 * index : 4 * index + 4, :], fields[index]], axis=0)
            for target in range(out_ref.shape[0]):
                out_ref[target, 8 * index : 8 * index + 8, :] = rows


def inverse_kernel(fields_ref, info_ref, table_ref, steep_ref, bend_ref, left_ref):
    @pl.when(pl.program_id(0) == 0)
    def _():
        inverse = (1.0 / info_ref[...]).T[:, 0:1]
        first, slope, laplace = [
            fields_ref[:, 8 * index : 8 * index + 8, :].reshape(ROWS, 2 * RINGS).T for index in range(3)
        ]
        scaled = first * inverse
        half = (0.5 * scaled) * inverse
        for index, rows in enumerate((slope, scaled, half, slope * inverse, 0.5 * laplace)):
            high = rows.astype(jnp.bfloat16)
            low = (rows - high.astype(jnp.float32)).astype(jnp.bfloat16)
            left_ref[index, :, 0:ROWS] = high
            left_ref[index, :, ROWS : 2 * ROWS] = low
            left_ref[index, :, 2 * ROWS :] = high

    chunk = 96
    base = pl.program_id(0) * RINGS
    for start in range(0, RINGS, chunk):
        rows_here = pl.ds(pl.multiple_of(base + start, chunk), chunk)

        def to_grid(rows, table):
            return jnp.dot(
                left_ref[rows, rows_here, :], table_ref[table], preferred_element_type=jnp.float32
            )

        p = to_grid(0, 0)
        q = to_grid(1, 1)
        half_t = to_grid(2, 2)
        s = to_grid(3, 1)
        half_l = to_grid(4, 0)
        p2, q2 = p * p, q * q
        outer = 1.0 + q2
        area = outer + p2
        root = lax.rsqrt(area)
        steep_ref[0, start : start + chunk, :] = (area * root).astype(jnp.bfloat16)
        top = (q2 - p2) * half_t - outer * half_l - (p * q) * s
        bend_ref[0, start : start + chunk, :] = (top * (root * root * root)).astype(jnp.bfloat16)


VMEM = pl.BlockSpec(memory_space=pltpu.VMEM)
SMEM = pl.BlockSpec(memory_space=pltpu.SMEM)


ANY = pl.BlockSpec(memory_space=pl.ANY)


COST = pl.CostEstimate(flops=1000000000, bytes_accessed=4000000, transcendentals=0)


def call(kernel, shape, dtype, in_specs, limit=24, **kwargs):
    return pl.pallas_call(
        kernel,
        out_shape=jax.ShapeDtypeStruct(shape, dtype),
        in_specs=in_specs,
        out_specs=VMEM,
        compiler_params=pltpu.CompilerParams(vmem_limit_bytes=limit << 20),
        **kwargs,
    )


def on_device(altitude_grids, polynomial_values, span_azimuthal_modes, slot_mapping):
    layers, rings, meridians = altitude_grids.shape
    n_ord = lax.axis_size("ord")
    modes, mapping = span_azimuthal_modes[None, :], slot_mapping[None, :]

    wave, info, orders, held = pl.pallas_call(
        prepare_kernel,
        out_shape=[
            jax.ShapeDtypeStruct((ROWS, meridians), jnp.bfloat16),
            jax.ShapeDtypeStruct((8, layers * rings), jnp.float32),
            jax.ShapeDtypeStruct((ROWS, 128), jnp.int32),
            jax.ShapeDtypeStruct(polynomial_values.shape, jnp.bfloat16),
        ],
        in_specs=[ANY] * 3,
        out_specs=[VMEM] * 4,
        scratch_shapes=[
            pltpu.VMEM((2, 1, BAND), jnp.int32),
            pltpu.SemaphoreType.DMA((2,)),
            pltpu.SemaphoreType.DMA((8,)),
        ],
        compiler_params=pltpu.CompilerParams(vmem_limit_bytes=40 << 20),
    )(modes, mapping, polynomial_values)
    product = call(forward_kernel, (ROWS, layers * rings), jnp.float32, [VMEM] * 2)(
        wave, altitude_grids
    )
    parts = lax.all_to_all(product.reshape(n_ord, 8, layers * rings), "ord", 0, 0, tiled=True)

    def analysis(which):
        return call(
            functools.partial(analysis_kernel, which), (4, PADDED), jnp.float32, [VMEM] * 3
        )(parts, info, held)

    outgoing = analysis(1)
    other = swap(outgoing, "lat", 1)
    coeffs = analysis(0) + other
    tables = call(table_kernel, (3, 3 * ROWS, meridians), jnp.bfloat16, [VMEM, ANY], cost_estimate=COST)(
        orders, outgoing
    )

    def turn(value, step):
        n = lax.axis_size("lat")
        return lax.ppermute(value, "lat", [(k, k // 8 * 8 + (k + 2 * step) % 8) for k in range(n)])

    received = [turn(coeffs, step) for step in (1, 3, 2)]
    coeffs = call(add_kernel, (4, PADDED), jnp.float32, [VMEM] * 4 + [ANY])(
        coeffs, *received, tables
    )
    coeffs = coeffs + swap(coeffs, "lat", 8)
    other = swap(coeffs, "lat", 1)

    mine = call(
        functools.partial(synthesis_kernel, 0), (12, layers * rings), jnp.float32, [VMEM] * 3
    )(coeffs, info, held)
    fields = call(
        functools.partial(synthesis_kernel, 1),
        (n_ord, 24, layers * rings),
        jnp.float32,
        [VMEM] * 4 + [ANY],
    )(other, info, held, mine, tables)
    everything = lax.all_to_all(fields, "ord", 0, 0, tiled=True)

    block = pl.BlockSpec((1, rings, meridians), lambda f: (f, 0, 0))
    return pl.pallas_call(
        inverse_kernel,
        grid=(layers,),
        out_shape=[jax.ShapeDtypeStruct((layers, rings, meridians), jnp.bfloat16)] * 2,
        in_specs=[VMEM] * 3,
        out_specs=[block, block],
        scratch_shapes=[pltpu.VMEM((5, layers * rings, 3 * ROWS), jnp.bfloat16)],
        compiler_params=pltpu.CompilerParams(vmem_limit_bytes=32 << 20),
    )(everything, info, tables)


def solution(mesh):
    return jax.shard_map(
        on_device,
        mesh=mesh,
        in_specs=(P(None, "lat", "ord"), P("ord", "lat", None), P(), P()),
        out_specs=(P(None, "lat", "ord"), P(None, "lat", "ord")),
        check_vma=False,
    )
```

```python
import functools
import math

import jax
import jax.numpy as jnp
from jax import lax
from jax.experimental import pallas as pl
from jax.experimental.pallas import tpu as pltpu
from jax.sharding import PartitionSpec as P

LMAX = 10800
MERIDIAN_AMOUNT = 21600
BAND = 64
NLAT = 10801
PACK = 10802
PADDED = 10880
WHOLE = 10752
RINGS = 192
MERIDIANS = 1350
ROWS = 2 * BAND
STEPS = (0, 2, 1, 3)
MASKS = (0, 3, 1, 2)

SINE_SERIES = tuple(
    (-1.0) ** n * (2.0 * math.pi) ** (2 * n + 1) / math.factorial(2 * n + 1) for n in range(8)
)


def swap(value, axis, mask):
    return lax.ppermute(value, axis, [(k, k ^ mask) for k in range(lax.axis_size(axis))])


def row_orders(modes, mapping, slot):
    lane = lax.broadcasted_iota(jnp.int32, (slot.shape[0], BAND), 1)
    entry = jnp.sum(
        jnp.where(lane == slot, mapping.astype(jnp.float32), 0.0), axis=1, keepdims=True
    ).astype(jnp.int32)
    return jnp.sum(
        jnp.where(lane == entry, modes.astype(jnp.float32), 0.0), axis=1, keepdims=True
    ).astype(jnp.int32)


def sine_turns(v):
    square = v * v
    total = SINE_SERIES[-1]
    for coefficient in SINE_SERIES[-2::-1]:
        total = total * square + coefficient
    return v * total


def cosine_of(orders, quarter, first):
    longitude = first + lax.broadcasted_iota(jnp.int32, (1, MERIDIANS), 1)
    product = orders * longitude
    cycles = (product.astype(jnp.float32) * (1.0 / MERIDIAN_AMOUNT)).astype(jnp.int32)
    turns = (product - cycles * MERIDIAN_AMOUNT + quarter * (MERIDIAN_AMOUNT // 4)).astype(
        jnp.float32
    ) * (1.0 / MERIDIAN_AMOUNT)
    turns = turns - jnp.round(turns)
    return sine_turns(0.25 - jnp.abs(turns))


def entry(values, index):
    return jnp.where(
        index >= 2,
        jnp.where(index == 2, values[2], values[3]),
        jnp.where(index == 0, values[0], values[1]),
    )


def prepare_kernel(small_ref, wave_ref, info_ref, orders_ref):
    ord_index, lat_index = lax.axis_index("ord"), lax.axis_index("lat")
    core = lat_index % 2
    modes, mapping = small_ref[0:1, :], small_ref[1:2, :]
    row = lax.broadcasted_iota(jnp.int32, (ROWS, 1), 0)
    step_y, step_z = entry(STEPS, row // 32), entry(STEPS, (row // 8) % 4)
    target = (ord_index // 4 ^ entry(MASKS, (row // 8) % 4)) * 4 + (ord_index + step_y) % 4
    orders = row_orders(modes, mapping, target * 4 + (row // 2) % 4)
    wave = cosine_of(orders, row % 2, ord_index * MERIDIANS)
    wave_ref[...] = (wave * (1.0 / math.sqrt(MERIDIAN_AMOUNT))).astype(jnp.bfloat16)
    source = (ord_index // 4 + 4 - step_z) % 4 * 4 + (ord_index + 4 - step_y) % 4
    slot = source * 4 + ((row // 4) % 2 + core) % 2 * 2 + (row // 2) % 2
    orders_ref[...] = jnp.broadcast_to(row_orders(modes, mapping, slot), (ROWS, 128))

    row = lax.broadcasted_iota(jnp.int32, (8, 1), 0)
    slot = ord_index * 4 + (core + row) % 2 * 2
    first_orders = row_orders(modes, mapping, slot).astype(jnp.float32)
    lane = lax.broadcasted_iota(jnp.int32, (8, 2 * RINGS), 1)
    cycle = lat_index * RINGS + jnp.where(lane >= RINGS, lane - RINGS, lane)
    v = (0.5 * (16 * RINGS - 1) - cycle.astype(jnp.float32)) * (0.5 / NLAT)
    sine, cosine = sine_turns(0.25 - jnp.abs(v)), sine_turns(v)
    info_ref[...] = jnp.where(row == 0, sine, jnp.where(row == 1, cosine, first_orders))


def forward_kernel(wave_ref, grids_ref, *out_refs):
    lines = grids_ref[...].reshape(2 * RINGS, MERIDIANS)
    product = lax.dot_general(
        wave_ref[...], lines, (((1,), (1,)), ((), ())), preferred_element_type=jnp.float32
    )
    for index, ref in enumerate(out_refs):
        ref[...] = product[32 * index : 32 * index + 32, :]


def hold_kernel(which, table_ref, _, held_ref, sems):
    pair = (lax.axis_index("lat") + which) % 2
    copies = []
    for block in range(4):
        rows = pl.ds(block * (RINGS // 4), RINGS // 4)
        copies.append(
            pltpu.make_async_copy(table_ref.at[pair, rows, :], held_ref.at[rows, :], sems.at[block])
        )
    for copy in copies:
        copy.start()
    for copy in copies:
        copy.wait()


def gather_kernel(first_ref, second_ref, third_ref, fourth_ref, _, keep_ref, send_ref):
    total = (first_ref[...] + second_ref[...]) + (third_ref[...] + fourth_ref[...])
    keep_ref[...], send_ref[...] = total[:16], total[16:]


def halve_kernel(first_ref, second_ref, _, keep_ref, send_ref):
    total = first_ref[...] + second_ref[...]
    keep_ref[...], send_ref[...] = total[:8], total[8:]


def table_kernel(orders_ref, after_ref, out_ref):
    row = lax.broadcasted_iota(jnp.int32, (ROWS, 1), 0)
    first = lax.axis_index("ord") * MERIDIANS
    orders = orders_ref[:, 0:1]
    fraction = orders.astype(jnp.float32) * (1.0 / LMAX)
    wave = cosine_of(orders, row % 2, first) * (1.0 / math.sqrt(BAND))
    turned = cosine_of(orders, row % 2 + 1, first) * (1.0 / math.sqrt(BAND))
    for index, table in enumerate((wave, fraction * turned, fraction * fraction * wave)):
        rounded = table.astype(jnp.bfloat16)
        out_ref[index, 0:ROWS, :] = rounded
        out_ref[index, ROWS:, :] = rounded


def analysis_kernel(which, first_ref, second_ref, info_ref, table_ref, out_ref):
    pair = (lax.axis_index("lat") + which) % 2
    first_len = LMAX + 1 - info_ref[2 + which : 3 + which, 0:1].astype(jnp.int32)
    total = first_ref[...] + second_ref[...]
    weighted = total * (info_ref[0:1, :] * (1.0 / math.sqrt(16 * RINGS)))
    mine = jnp.where(pair == 1, weighted[4:8], weighted[0:4])
    left, right = mine[:, :RINGS], mine[:, RINGS:]
    rows = jnp.concatenate([left[0:2], right[0:2], left[2:4], right[2:4]], axis=0).astype(
        jnp.bfloat16
    )
    step = 1536
    for start in range(0, PACK, step):
        size = min(step, PACK - start)
        product = jnp.dot(
            rows, table_ref[:, start : start + size], preferred_element_type=jnp.float32
        )
        position = start + lax.broadcasted_iota(jnp.int32, (4, size), 1)
        out_ref[:, start : start + size] = jnp.where(
            position >= first_len, product[4:8], product[0:4]
        )
    out_ref[:, PACK:] = jnp.zeros((4, PADDED - PACK), jnp.float32)


def add_kernel(first_ref, second_ref, third_ref, fourth_ref, _, out_ref):
    out_ref[...] = (first_ref[...] + second_ref[...]) + (third_ref[...] + fourth_ref[...])


def synthesis_kernel(which, coeffs_ref, info_ref, table_ref, *rest):
    order = info_ref[2 + which : 3 + which, 0:1].astype(jnp.int32)
    row = lax.broadcasted_iota(jnp.int32, (8, 1), 0)
    upper = (row // 2) % 2 == 1
    first_len = LMAX + 1 - order
    base = jnp.where(upper, -1, order)
    own_order = jnp.where(upper, LMAX - order, order)
    length = jnp.where(upper, order + 1, first_len).astype(jnp.float32)
    begin = jnp.where(upper, first_len, 0)
    end = jnp.where(upper, PACK, first_len)
    scaling = 1.0 / jnp.sqrt(length)
    step = 1536
    synth = jnp.zeros((32, RINGS), jnp.float32)
    for start in range(0, PADDED, step):
        size = min(step, PADDED - start)
        own = coeffs_ref[:, start : start + size]
        if start + size < PADDED:
            ahead = coeffs_ref[:, start + size : start + size + 128]
        else:
            ahead = jnp.zeros((4, 128), jnp.float32)
        wide = jnp.concatenate([own, ahead], axis=1)
        after = pltpu.roll(wide, size + 127, axis=1)[:, :size]
        spread = [jnp.concatenate([a[0:2], a[0:2], a[2:4], a[2:4]], axis=0) for a in (own, after)]
        position = start + lax.broadcasted_iota(jnp.int32, (8, size), 1)
        inside = (position >= begin) & (position < end)
        degree = (base + position).astype(jnp.float32)
        plain = jnp.where(inside, scaling, 0.0)
        sloped = plain * (degree * (1.0 / LMAX))
        ahead_factor = jnp.where(
            inside & (position < end - 1),
            (degree + (1.0 + own_order.astype(jnp.float32))) * (scaling * (1.0 / LMAX)),
            0.0,
        )
        curved = sloped * ((degree + 1.0) * (1.0 / LMAX))
        weights = jnp.concatenate(
            [spread[0] * plain, spread[0] * sloped, spread[1] * ahead_factor, spread[0] * curved],
            axis=0,
        ).astype(jnp.bfloat16)
        held = min(size, PACK - start)
        synth = synth + lax.dot_general(
            weights[:, :held],
            table_ref[:, start : start + held],
            (((1,), (1,)), ((), ())),
            preferred_element_type=jnp.float32,
        )
    sine, cosine = info_ref[0:1, :RINGS], info_ref[1:2, :RINGS]
    fields = [synth[0:8], (cosine * synth[8:16] - synth[16:24]) / sine, synth[24:32]]
    fields = [jnp.concatenate([a[0:4], a[4:8]], axis=1) for a in fields]
    if which == 0:
        (out_ref,) = rest
        for index in range(3):
            out_ref[4 * index : 4 * index + 4, :] = fields[index]
    else:
        other_ref, _, out_ref = rest
        for index in range(3):
            rows = jnp.concatenate([other_ref[4 * index : 4 * index + 4, :], fields[index]], axis=0)
            out_ref[8 * index : 8 * index + 8, :] = rows


def inverse_kernel(*refs):
    blocks, (info_ref, table_ref, steep_ref, bend_ref, left_ref) = refs[:4], refs[4:]

    @pl.when(pl.program_id(0) == 0)
    def _():
        inverse = (1.0 / info_ref[...]).T[:, 0:1]
        first, slope, laplace = [
            jnp.concatenate(
                [ref[:, 8 * index : 8 * index + 8, :].reshape(ROWS // 4, 2 * RINGS) for ref in blocks],
                axis=0,
            ).T
            for index in range(3)
        ]
        scaled = first * inverse
        half = (0.5 * scaled) * inverse
        for index, rows in enumerate((slope, scaled, half, slope * inverse, 0.5 * laplace)):
            high = rows.astype(jnp.bfloat16)
            low = (rows - high.astype(jnp.float32)).astype(jnp.bfloat16)
            left_ref[index, :, 0:ROWS] = high
            left_ref[index, :, ROWS:] = low

    rows_here = pl.ds(pl.multiple_of(pl.program_id(0) * RINGS, RINGS), RINGS)

    def to_grid(rows, table):
        return jnp.dot(
            left_ref[rows, rows_here, :], table_ref[table], preferred_element_type=jnp.float32
        )

    p = to_grid(0, 0)
    q = to_grid(1, 1)
    half_t = to_grid(2, 2)
    s = to_grid(3, 1)
    half_l = to_grid(4, 0)
    p2, q2 = p * p, q * q
    outer = 1.0 + q2
    area = outer + p2
    root = lax.rsqrt(area)
    steep_ref[0] = (area * root).astype(jnp.bfloat16)
    top = (q2 - p2) * half_t - outer * half_l - (p * q) * s
    bend_ref[0] = (top * (root * root * root)).astype(jnp.bfloat16)


VMEM = pl.BlockSpec(memory_space=pltpu.VMEM)
SMEM = pl.BlockSpec(memory_space=pltpu.SMEM)


ANY = pl.BlockSpec(memory_space=pl.ANY)


COST = pl.CostEstimate(flops=1000000000, bytes_accessed=4000000, transcendentals=0)


def call(kernel, shape, dtype, in_specs, limit=24, **kwargs):
    return pl.pallas_call(
        kernel,
        out_shape=jax.ShapeDtypeStruct(shape, dtype),
        in_specs=in_specs,
        out_specs=VMEM,
        compiler_params=pltpu.CompilerParams(vmem_limit_bytes=limit << 20),
        **kwargs,
    )


def on_device(altitude_grids, polynomial_values, span_azimuthal_modes, slot_mapping):
    layers, rings, meridians = altitude_grids.shape
    n_ord = lax.axis_size("ord")
    lines = layers * rings

    def from_back(value, stride, step):
        size = 4 * stride
        return lax.ppermute(
            value, "ord", [(k, k // size * size + (k + stride * step) % size) for k in range(n_ord)]
        )

    wave, info, orders = pl.pallas_call(
        prepare_kernel,
        out_shape=[
            jax.ShapeDtypeStruct((ROWS, meridians), jnp.bfloat16),
            jax.ShapeDtypeStruct((8, lines), jnp.float32),
            jax.ShapeDtypeStruct((ROWS, 128), jnp.int32),
        ],
        in_specs=[VMEM],
        out_specs=[VMEM] * 3,
        cost_estimate=COST,
        compiler_params=pltpu.CompilerParams(vmem_limit_bytes=24 << 20),
    )(jnp.stack([span_azimuthal_modes, slot_mapping]))
    product = pl.pallas_call(
        forward_kernel,
        out_shape=[jax.ShapeDtypeStruct((32, lines), jnp.float32)] * 4,
        in_specs=[VMEM] * 2,
        out_specs=[VMEM] * 4,
        compiler_params=pltpu.CompilerParams(vmem_limit_bytes=24 << 20),
    )(wave, altitude_grids)
    parts = [product[0]] + [from_back(product[a], 1, STEPS[a]) for a in (1, 2, 3)]

    def hold(which, after):
        return call(
            functools.partial(hold_kernel, which),
            polynomial_values.shape[1:],
            jnp.bfloat16,
            [ANY, ANY],
            limit=44,
            cost_estimate=COST,
            scratch_shapes=[pltpu.SemaphoreType.DMA((4,))],
        )(polynomial_values, after)

    def summed(kernel, rows, values, after):
        return pl.pallas_call(
            kernel,
            out_shape=[jax.ShapeDtypeStruct((rows, lines), jnp.float32)] * 2,
            in_specs=[VMEM] * len(values) + [ANY],
            out_specs=[VMEM] * 2,
            compiler_params=pltpu.CompilerParams(vmem_limit_bytes=24 << 20),
        )(*values, after)

    other_table = hold(1, info)
    keep, send = summed(gather_kernel, 16, parts, other_table)
    own_table = hold(0, keep)
    keep, send = summed(halve_kernel, 8, [keep, swap(send, "ord", 4)], own_table)
    parts = [keep, swap(send, "ord", 12)]
    tables_held = (own_table, other_table)

    def analysis(which):
        return call(
            functools.partial(analysis_kernel, which), (4, PADDED), jnp.float32, [VMEM] * 4
        )(*parts, info, tables_held[which])

    outgoing = analysis(1)
    other = swap(outgoing, "lat", 1)
    coeffs = analysis(0) + other
    tables = call(table_kernel, (3, 2 * ROWS, meridians), jnp.bfloat16, [VMEM, ANY], cost_estimate=COST)(
        orders, outgoing
    )

    def turn(value, step):
        n = lax.axis_size("lat")
        return lax.ppermute(value, "lat", [(k, k // 8 * 8 + (k + 2 * step) % 8) for k in range(n)])

    received = [turn(coeffs, step) for step in STEPS[1:]]
    coeffs = call(add_kernel, (4, PADDED), jnp.float32, [VMEM] * 4 + [ANY])(
        coeffs, *received, tables
    )
    coeffs = coeffs + swap(coeffs, "lat", 8)
    other = swap(coeffs, "lat", 1)

    mine = call(
        functools.partial(synthesis_kernel, 0), (12, layers * rings), jnp.float32, [VMEM] * 3
    )(coeffs, info, own_table)
    fields = call(
        functools.partial(synthesis_kernel, 1),
        (24, layers * rings),
        jnp.float32,
        [VMEM] * 4 + [ANY],
    )(other, info, other_table, mine, tables)

    column = jnp.stack([fields] + [from_back(fields, 4, step) for step in STEPS[1:]])
    blocks = [column] + [from_back(column, 1, step) for step in STEPS[1:]]

    block = pl.BlockSpec((1, rings, meridians), lambda f: (f, 0, 0))
    return pl.pallas_call(
        inverse_kernel,
        grid=(layers,),
        out_shape=[jax.ShapeDtypeStruct((layers, rings, meridians), jnp.bfloat16)] * 2,
        in_specs=[VMEM] * 6,
        out_specs=[block, block],
        scratch_shapes=[pltpu.VMEM((5, layers * rings, 2 * ROWS), jnp.bfloat16)],
        compiler_params=pltpu.CompilerParams(vmem_limit_bytes=32 << 20),
    )(*blocks, info, tables)


def solution(mesh):
    return jax.shard_map(
        on_device,
        mesh=mesh,
        in_specs=(P(None, "lat", "ord"), P("ord", "lat", None), P(), P()),
        out_specs=(P(None, "lat", "ord"), P(None, "lat", "ord")),
        check_vma=False,
    )
```

```python
import functools
import math

import jax
import jax.numpy as jnp
from jax import lax
from jax.experimental import pallas as pl
from jax.experimental.pallas import tpu as pltpu
from jax.sharding import PartitionSpec as P

LMAX = 10800
MERIDIAN_AMOUNT = 21600
BAND = 64
NLAT = 10801
PACK = 10802
PADDED = 10880
WHOLE = 10752
RINGS = 192
MERIDIANS = 1350
ROWS = 2 * BAND
STEPS = (0, 2, 1, 3)
MASKS = (0, 3, 1, 2)

SINE_SERIES = tuple(
    (-1.0) ** n * (2.0 * math.pi) ** (2 * n + 1) / math.factorial(2 * n + 1) for n in range(7)
)


def swap(value, axis, mask):
    return lax.ppermute(value, axis, [(k, k ^ mask) for k in range(lax.axis_size(axis))])


def row_orders(modes, mapping, slot):
    lane = lax.broadcasted_iota(jnp.int32, (slot.shape[0], BAND), 1)
    entry = jnp.sum(
        jnp.where(lane == slot, mapping.astype(jnp.float32), 0.0), axis=1, keepdims=True
    ).astype(jnp.int32)
    return jnp.sum(
        jnp.where(lane == entry, modes.astype(jnp.float32), 0.0), axis=1, keepdims=True
    ).astype(jnp.int32)


def sine_turns(v):
    square = v * v
    total = SINE_SERIES[-1]
    for coefficient in SINE_SERIES[-2::-1]:
        total = total * square + coefficient
    return v * total


def cosine_of(orders, quarter, block):
    longitude = lax.broadcasted_iota(jnp.int32, (1, MERIDIANS), 1).astype(jnp.float32)
    begin = (orders * (block * MERIDIANS)) % MERIDIAN_AMOUNT + quarter * (MERIDIAN_AMOUNT // 4)
    product = orders.astype(jnp.float32) * longitude
    cycles = jnp.round(product * (1.0 / MERIDIAN_AMOUNT))
    rest = (product - cycles * MERIDIAN_AMOUNT) + begin.astype(jnp.float32)
    turns = rest * (1.0 / MERIDIAN_AMOUNT)
    return sine_turns(0.25 - jnp.abs(turns - jnp.round(turns)))


def entry(values, index):
    return jnp.where(
        index >= 2,
        jnp.where(index == 2, values[2], values[3]),
        jnp.where(index == 0, values[0], values[1]),
    )


def prepare_kernel(small_ref, wave_ref):
    ord_index = lax.axis_index("ord")
    row = lax.broadcasted_iota(jnp.int32, (ROWS, 1), 0)
    target = (ord_index // 4 ^ entry(MASKS, (row // 8) % 4)) * 4 + (
        ord_index + entry(STEPS, row // 32)
    ) % 4
    orders = row_orders(small_ref[0:1, :], small_ref[1:2, :], target * 4 + (row // 2) % 4)
    wave = cosine_of(orders, row % 2, ord_index)
    wave_ref[...] = (wave * (1.0 / math.sqrt(MERIDIAN_AMOUNT))).astype(jnp.bfloat16)


def info_kernel(small_ref, _, info_ref, orders_ref):
    ord_index, lat_index = lax.axis_index("ord"), lax.axis_index("lat")
    core = lat_index % 2
    modes, mapping = small_ref[0:1, :], small_ref[1:2, :]
    row = lax.broadcasted_iota(jnp.int32, (ROWS, 1), 0)
    step_y, step_z = entry(STEPS, row // 32), entry(STEPS, (row // 8) % 4)
    source = (ord_index // 4 + 4 - step_z) % 4 * 4 + (ord_index + 4 - step_y) % 4
    slot = source * 4 + ((row // 4) % 2 + core) % 2 * 2 + (row // 2) % 2
    orders_ref[...] = jnp.broadcast_to(row_orders(modes, mapping, slot), (ROWS, 128))

    row = lax.broadcasted_iota(jnp.int32, (8, 1), 0)
    slot = ord_index * 4 + (core + row) % 2 * 2
    first_orders = row_orders(modes, mapping, slot).astype(jnp.float32)
    lane = lax.broadcasted_iota(jnp.int32, (8, 2 * RINGS), 1)
    cycle = lat_index * RINGS + jnp.where(lane >= RINGS, lane - RINGS, lane)
    v = (0.5 * (16 * RINGS - 1) - cycle.astype(jnp.float32)) * (0.5 / NLAT)
    sine, cosine = sine_turns(0.25 - jnp.abs(v)), sine_turns(v)
    info_ref[...] = jnp.where(row == 0, sine, jnp.where(row == 1, cosine, first_orders))


def forward_kernel(wave_ref, grids_ref, *out_refs):
    lines = grids_ref[...].reshape(2 * RINGS, MERIDIANS)
    product = lax.dot_general(
        wave_ref[...], lines, (((1,), (1,)), ((), ())), preferred_element_type=jnp.float32
    )
    for index, ref in enumerate(out_refs):
        ref[...] = product[32 * index : 32 * index + 32, :]


def hold_kernel(which, table_ref, _, held_ref, sems):
    pair = (lax.axis_index("lat") + which) % 2
    copies = []
    for block in range(4):
        rows = pl.ds(block * (RINGS // 4), RINGS // 4)
        copies.append(
            pltpu.make_async_copy(table_ref.at[pair, rows, :], held_ref.at[rows, :], sems.at[block])
        )
    for copy in copies:
        copy.start()
    for copy in copies:
        copy.wait()


def gather_kernel(first_ref, second_ref, third_ref, fourth_ref, _, keep_ref, send_ref):
    total = (first_ref[...] + second_ref[...]) + (third_ref[...] + fourth_ref[...])
    keep_ref[...], send_ref[...] = total[:16], total[16:]


def halve_kernel(first_ref, second_ref, _, keep_ref, send_ref):
    total = first_ref[...] + second_ref[...]
    keep_ref[...], send_ref[...] = total[:8], total[8:]


def table_kernel(orders_ref, after_ref, out_ref):
    row = lax.broadcasted_iota(jnp.int32, (ROWS, 1), 0)
    first = lax.axis_index("ord")
    orders = orders_ref[:, 0:1]
    fraction = orders.astype(jnp.float32) * (1.0 / LMAX)
    wave = cosine_of(orders, row % 2, first) * (1.0 / math.sqrt(BAND))
    turned = cosine_of(orders, row % 2 + 1, first) * (1.0 / math.sqrt(BAND))
    for index, table in enumerate((wave, fraction * turned, fraction * fraction * wave)):
        rounded = table.astype(jnp.bfloat16)
        out_ref[index, 0:ROWS, :] = rounded
        out_ref[index, ROWS:, :] = rounded


def analysis_kernel(which, first_ref, second_ref, info_ref, table_ref, out_ref):
    pair = (lax.axis_index("lat") + which) % 2
    first_len = LMAX + 1 - info_ref[2 + which : 3 + which, 0:1].astype(jnp.int32)
    total = first_ref[...] + second_ref[...]
    weighted = total * (info_ref[0:1, :] * (1.0 / math.sqrt(16 * RINGS)))
    mine = jnp.where(pair == 1, weighted[4:8], weighted[0:4])
    left, right = mine[:, :RINGS], mine[:, RINGS:]
    rows = jnp.concatenate([left[0:2], right[0:2], left[2:4], right[2:4]], axis=0).astype(
        jnp.bfloat16
    )
    step = 1536
    for start in range(0, PACK, step):
        size = min(step, PACK - start)
        product = jnp.dot(
            rows, table_ref[:, start : start + size], preferred_element_type=jnp.float32
        )
        position = start + lax.broadcasted_iota(jnp.int32, (4, size), 1)
        out_ref[:, start : start + size] = jnp.where(
            position >= first_len, product[4:8], product[0:4]
        )
    out_ref[:, PACK:] = jnp.zeros((4, PADDED - PACK), jnp.float32)


def turn_kernel(own_ref, other_ref, _, own_out_ref, other_out_ref):
    step = 1536
    for table_ref, out_ref in ((own_ref, own_out_ref), (other_ref, other_out_ref)):
        for start in range(0, WHOLE, step):
            out_ref[start : start + step, :] = table_ref[:, start : start + step].T
        rest = jnp.concatenate(
            [table_ref[:, WHOLE:], jnp.zeros((RINGS, PADDED - PACK), jnp.bfloat16)], axis=1
        )
        out_ref[WHOLE:, :] = rest.T


def add_kernel(first_ref, second_ref, *rest):
    out_ref = rest[-1]
    out_ref[...] = first_ref[...] + second_ref[...]


def factor_kernel(which, info_ref, _, out_ref):
    order = info_ref[2 + which : 3 + which, 0:1].astype(jnp.int32)
    row = lax.broadcasted_iota(jnp.int32, (8, 1), 0)
    upper = (row // 2) % 2 == 1
    first_len = LMAX + 1 - order
    base = jnp.where(upper, -1, order)
    own_order = jnp.where(upper, LMAX - order, order).astype(jnp.float32)
    length = jnp.where(upper, order + 1, first_len).astype(jnp.float32)
    begin = jnp.where(upper, first_len, 0)
    end = jnp.where(upper, PACK, first_len)
    scaling = 1.0 / jnp.sqrt(length)
    step = 1536
    for start in range(0, PADDED, step):
        size = min(step, PADDED - start)
        position = start + lax.broadcasted_iota(jnp.int32, (8, size), 1)
        inside = (position >= begin) & (position < end)
        degree = (base + position).astype(jnp.float32)
        plain = jnp.where(inside, scaling, 0.0)
        sloped = plain * (degree * (1.0 / LMAX))
        out_ref[0, :, start : start + size] = plain
        out_ref[1, :, start : start + size] = sloped
        out_ref[2, :, start : start + size] = jnp.where(
            inside & (position < end - 1),
            (degree + (1.0 + own_order)) * (scaling * (1.0 / LMAX)),
            0.0,
        )
        out_ref[3, :, start : start + size] = sloped * ((degree + 1.0) * (1.0 / LMAX))


def synthesis_kernel(which, coeffs_ref, info_ref, table_ref, factor_ref, *rest):
    step = 1536
    synth = jnp.zeros((32, RINGS), jnp.float32)
    for start in range(0, PADDED, step):
        size = min(step, PADDED - start)
        own = coeffs_ref[:, start : start + size]
        if start + size < PADDED:
            ahead = coeffs_ref[:, start + size : start + size + 128]
        else:
            ahead = jnp.zeros((4, 128), jnp.float32)
        wide = jnp.concatenate([own, ahead], axis=1)
        after = pltpu.roll(wide, size + 127, axis=1)[:, :size]
        own, after = [
            jnp.concatenate([a[0:2], a[0:2], a[2:4], a[2:4]], axis=0) for a in (own, after)
        ]
        weights = jnp.concatenate(
            [
                (after if index == 2 else own) * factor_ref[index, :, start : start + size]
                for index in range(4)
            ],
            axis=0,
        ).astype(jnp.bfloat16)
        synth = synth + jnp.dot(
            weights, table_ref[start : start + size, :], preferred_element_type=jnp.float32
        )
    sine, cosine = info_ref[0:1, :RINGS], info_ref[1:2, :RINGS]
    fields = [synth[0:8], (cosine * synth[8:16] - synth[16:24]) / sine, synth[24:32]]
    fields = [jnp.concatenate([a[0:4], a[4:8]], axis=1) for a in fields]
    if which == 0:
        (out_ref,) = rest
        for index in range(3):
            out_ref[4 * index : 4 * index + 4, :] = fields[index]
    else:
        other_ref, _, out_ref = rest
        for index in range(3):
            rows = jnp.concatenate([other_ref[4 * index : 4 * index + 4, :], fields[index]], axis=0)
            out_ref[8 * index : 8 * index + 8, :] = rows


def inverse_kernel(*refs):
    blocks, (info_ref, table_ref, steep_ref, bend_ref, left_ref) = refs[:4], refs[4:]

    @pl.when(pl.program_id(0) == 0)
    def _():
        inverse = (1.0 / info_ref[...]).T[:, 0:1]
        first, slope, laplace = [
            jnp.concatenate(
                [ref[:, 8 * index : 8 * index + 8, :].reshape(ROWS // 4, 2 * RINGS) for ref in blocks],
                axis=0,
            ).T
            for index in range(3)
        ]
        scaled = first * inverse
        half = (0.5 * scaled) * inverse
        for index, rows in enumerate((slope, 0.5 * laplace, scaled, slope * inverse, half)):
            high = rows.astype(jnp.bfloat16)
            low = (rows - high.astype(jnp.float32)).astype(jnp.bfloat16)
            for layer in range(2):
                here = slice(layer * RINGS, (layer + 1) * RINGS)
                there = slice(index * RINGS, (index + 1) * RINGS)
                left_ref[layer, there, 0:ROWS] = high[here]
                left_ref[layer, there, ROWS:] = low[here]

    def to_grids(first, count, table):
        rows = left_ref[pl.program_id(0), first * RINGS : (first + count) * RINGS, :]
        product = jnp.dot(rows, table_ref[table], preferred_element_type=jnp.float32)
        return [product[index * RINGS : (index + 1) * RINGS] for index in range(count)]

    p, half_l = to_grids(0, 2, 0)
    q, s = to_grids(2, 2, 1)
    (half_t,) = to_grids(4, 1, 2)
    p2, q2 = p * p, q * q
    outer = 1.0 + q2
    area = outer + p2
    root = lax.rsqrt(area)
    steep_ref[0] = (area * root).astype(jnp.bfloat16)
    top = (q2 - p2) * half_t - outer * half_l - (p * q) * s
    bend_ref[0] = (top * (root * root * root)).astype(jnp.bfloat16)


VMEM = pl.BlockSpec(memory_space=pltpu.VMEM)
SMEM = pl.BlockSpec(memory_space=pltpu.SMEM)


ANY = pl.BlockSpec(memory_space=pl.ANY)


COST = pl.CostEstimate(flops=1000000000, bytes_accessed=4000000, transcendentals=0)


def call(kernel, shape, dtype, in_specs, limit=24, **kwargs):
    return pl.pallas_call(
        kernel,
        out_shape=jax.ShapeDtypeStruct(shape, dtype),
        in_specs=in_specs,
        out_specs=VMEM,
        compiler_params=pltpu.CompilerParams(vmem_limit_bytes=limit << 20),
        **kwargs,
    )


def on_device(altitude_grids, polynomial_values, span_azimuthal_modes, slot_mapping):
    layers, rings, meridians = altitude_grids.shape
    n_ord = lax.axis_size("ord")
    lines = layers * rings

    def from_back(value, stride, step):
        size = 4 * stride
        return lax.ppermute(
            value, "ord", [(k, k // size * size + (k + stride * step) % size) for k in range(n_ord)]
        )

    small = jnp.stack([span_azimuthal_modes, slot_mapping])
    wave = call(prepare_kernel, (ROWS, meridians), jnp.bfloat16, [VMEM], cost_estimate=COST)(small)
    product = pl.pallas_call(
        forward_kernel,
        out_shape=[jax.ShapeDtypeStruct((32, lines), jnp.float32)] * 4,
        in_specs=[VMEM] * 2,
        out_specs=[VMEM] * 4,
        compiler_params=pltpu.CompilerParams(vmem_limit_bytes=24 << 20),
    )(wave, altitude_grids)
    info, orders = pl.pallas_call(
        info_kernel,
        out_shape=[
            jax.ShapeDtypeStruct((8, lines), jnp.float32),
            jax.ShapeDtypeStruct((ROWS, 128), jnp.int32),
        ],
        in_specs=[VMEM, ANY],
        out_specs=[VMEM] * 2,
        cost_estimate=COST,
        compiler_params=pltpu.CompilerParams(vmem_limit_bytes=24 << 20),
    )(small, product[0])
    parts = [product[0]] + [from_back(product[a], 1, STEPS[a]) for a in (1, 2, 3)]

    def hold(which, after):
        return call(
            functools.partial(hold_kernel, which),
            polynomial_values.shape[1:],
            jnp.bfloat16,
            [ANY, ANY],
            limit=44,
            cost_estimate=COST,
            scratch_shapes=[pltpu.SemaphoreType.DMA((4,))],
        )(polynomial_values, after)

    def summed(kernel, rows, values, after):
        return pl.pallas_call(
            kernel,
            out_shape=[jax.ShapeDtypeStruct((rows, lines), jnp.float32)] * 2,
            in_specs=[VMEM] * len(values) + [ANY],
            out_specs=[VMEM] * 2,
            compiler_params=pltpu.CompilerParams(vmem_limit_bytes=24 << 20),
        )(*values, after)

    other_table = hold(1, product[0])
    keep, send = summed(gather_kernel, 16, parts, other_table)
    own_table = hold(0, keep)
    keep, send = summed(halve_kernel, 8, [keep, swap(send, "ord", 4)], own_table)
    parts = [keep, swap(send, "ord", 12)]
    tables_held = (own_table, other_table)

    def analysis(which):
        return call(
            functools.partial(analysis_kernel, which), (4, PADDED), jnp.float32, [VMEM] * 4
        )(*parts, info, tables_held[which])

    outgoing = analysis(1)
    other = swap(outgoing, "lat", 1)
    coeffs = analysis(0) + other
    tables = call(table_kernel, (3, 2 * ROWS, meridians), jnp.bfloat16, [VMEM, ANY], cost_estimate=COST)(
        orders, outgoing
    )

    def exchanged(value, even, odd):
        n = lax.axis_size("lat")
        return lax.ppermute(value, "lat", [(k, k ^ (odd if k % 2 else even)) for k in range(n)])

    def summed_with(value, received, *done):
        return call(add_kernel, (4, PADDED), jnp.float32, [VMEM] * 2 + [ANY] * len(done))(
            value, received, *done
        )

    def factor(which, after):
        return call(
            functools.partial(factor_kernel, which),
            (4, 8, PADDED),
            jnp.float32,
            [VMEM, ANY],
            cost_estimate=COST,
        )(info, after)

    factors = [factor(which, coeffs) for which in (0, 1)]
    coeffs = summed_with(coeffs, exchanged(coeffs, 2, 6), *factors)
    coeffs = summed_with(coeffs, exchanged(coeffs, 6, 8), tables)
    own_turned, other_turned = pl.pallas_call(
        turn_kernel,
        out_shape=[jax.ShapeDtypeStruct((PADDED, rings), jnp.bfloat16)] * 2,
        in_specs=[VMEM, VMEM, ANY],
        out_specs=[VMEM] * 2,
        cost_estimate=COST,
        compiler_params=pltpu.CompilerParams(vmem_limit_bytes=24 << 20),
    )(own_table, other_table, coeffs)
    coeffs = summed_with(coeffs, exchanged(coeffs, 8, 2), own_turned, other_turned)
    other = swap(coeffs, "lat", 1)

    mine = call(
        functools.partial(synthesis_kernel, 0), (12, layers * rings), jnp.float32, [VMEM] * 4
    )(coeffs, info, own_turned, factors[0])
    fields = call(
        functools.partial(synthesis_kernel, 1),
        (24, layers * rings),
        jnp.float32,
        [VMEM] * 5 + [ANY],
    )(other, info, other_turned, factors[1], mine, tables)

    column = jnp.stack([fields] + [from_back(fields, 4, step) for step in STEPS[1:]])
    blocks = [column] + [from_back(column, 1, step) for step in STEPS[1:]]

    block = pl.BlockSpec((1, rings, meridians), lambda f: (f, 0, 0))
    return pl.pallas_call(
        inverse_kernel,
        grid=(layers,),
        out_shape=[jax.ShapeDtypeStruct((layers, rings, meridians), jnp.bfloat16)] * 2,
        in_specs=[VMEM] * 6,
        out_specs=[block, block],
        scratch_shapes=[pltpu.VMEM((layers, 5 * rings, 2 * ROWS), jnp.bfloat16)],
        compiler_params=pltpu.CompilerParams(vmem_limit_bytes=32 << 20),
    )(*blocks, info, tables)


def solution(mesh):
    return jax.shard_map(
        on_device,
        mesh=mesh,
        in_specs=(P(None, "lat", "ord"), P("ord", "lat", None), P(), P()),
        out_specs=(P(None, "lat", "ord"), P(None, "lat", "ord")),
        check_vma=False,
    )
```

```python
import functools
import math

import jax
import jax.numpy as jnp
from jax import lax
from jax.experimental import pallas as pl
from jax.experimental.pallas import tpu as pltpu
from jax.sharding import PartitionSpec as P

LMAX = 10800
MERIDIAN_AMOUNT = 21600
BAND = 64
NLAT = 10801
PACK = 10802
PADDED = 10880
WHOLE = 10752
RINGS = 192
MERIDIANS = 1350
ROWS = 2 * BAND
STEPS = (0, 2, 1, 3)
MASKS = (0, 3, 1, 2)
COLUMNS = 256

SINE_SERIES = tuple(
    (-1.0) ** n * (2.0 * math.pi) ** (2 * n + 1) / math.factorial(2 * n + 1) for n in range(7)
)


def swap(value, axis, mask):
    return lax.ppermute(value, axis, [(k, k ^ mask) for k in range(lax.axis_size(axis))])


def row_orders(modes, mapping, slot):
    lane = lax.broadcasted_iota(jnp.int32, (slot.shape[0], BAND), 1)
    entry = jnp.sum(
        jnp.where(lane == slot, mapping.astype(jnp.float32), 0.0), axis=1, keepdims=True
    ).astype(jnp.int32)
    return jnp.sum(
        jnp.where(lane == entry, modes.astype(jnp.float32), 0.0), axis=1, keepdims=True
    ).astype(jnp.int32)


def sine_turns(v):
    square = v * v
    total = SINE_SERIES[-1]
    for coefficient in SINE_SERIES[-2::-1]:
        total = total * square + coefficient
    return v * total


def cosine_of(orders, quarter, block):
    longitude = lax.broadcasted_iota(jnp.int32, (1, MERIDIANS), 1).astype(jnp.float32)
    begin = (orders * (block * MERIDIANS)) % MERIDIAN_AMOUNT + quarter * (MERIDIAN_AMOUNT // 4)
    product = orders.astype(jnp.float32) * longitude
    cycles = jnp.round(product * (1.0 / MERIDIAN_AMOUNT))
    rest = (product - cycles * MERIDIAN_AMOUNT) + begin.astype(jnp.float32)
    turns = rest * (1.0 / MERIDIAN_AMOUNT)
    return sine_turns(0.25 - jnp.abs(turns - jnp.round(turns)))


def entry(values, index):
    return jnp.where(
        index >= 2,
        jnp.where(index == 2, values[2], values[3]),
        jnp.where(index == 0, values[0], values[1]),
    )


def prepare_kernel(small_ref, wave_ref):
    ord_index = lax.axis_index("ord")
    row = lax.broadcasted_iota(jnp.int32, (ROWS, 1), 0)
    target = (ord_index // 4 ^ entry(MASKS, (row // 8) % 4)) * 4 + (
        ord_index + entry(STEPS, row // 32)
    ) % 4
    orders = row_orders(small_ref[0:1, :], small_ref[1:2, :], target * 4 + (row // 2) % 4)
    wave = cosine_of(orders, row % 2, ord_index)
    wave_ref[...] = (wave * (1.0 / math.sqrt(MERIDIAN_AMOUNT))).astype(jnp.bfloat16)


def info_kernel(small_ref, _, info_ref, orders_ref):
    ord_index, lat_index = lax.axis_index("ord"), lax.axis_index("lat")
    core = lat_index % 2
    modes, mapping = small_ref[0:1, :], small_ref[1:2, :]
    row = lax.broadcasted_iota(jnp.int32, (ROWS, 1), 0)
    step_y, step_z = entry(STEPS, row // 32), entry(STEPS, (row // 8) % 4)
    source = (ord_index // 4 + 4 - step_z) % 4 * 4 + (ord_index + 4 - step_y) % 4
    slot = source * 4 + ((row // 4) % 2 + core) % 2 * 2 + (row // 2) % 2
    orders_ref[...] = jnp.broadcast_to(row_orders(modes, mapping, slot), (ROWS, 128))

    row = lax.broadcasted_iota(jnp.int32, (8, 1), 0)
    slot = ord_index * 4 + (core + row) % 2 * 2
    first_orders = row_orders(modes, mapping, slot).astype(jnp.float32)
    lane = lax.broadcasted_iota(jnp.int32, (8, 2 * RINGS), 1)
    cycle = lat_index * RINGS + jnp.where(lane >= RINGS, lane - RINGS, lane)
    v = (0.5 * (16 * RINGS - 1) - cycle.astype(jnp.float32)) * (0.5 / NLAT)
    sine, cosine = sine_turns(0.25 - jnp.abs(v)), sine_turns(v)
    info_ref[...] = jnp.where(row == 0, sine, jnp.where(row == 1, cosine, first_orders))


def forward_kernel(wave_ref, grids_ref, *out_refs):
    lines = grids_ref[...].reshape(2 * RINGS, MERIDIANS)
    product = lax.dot_general(
        wave_ref[...], lines, (((1,), (1,)), ((), ())), preferred_element_type=jnp.float32
    )
    for index, ref in enumerate(out_refs):
        ref[...] = product[32 * index : 32 * index + 32, :]


def hold_kernel(which, table_ref, _, held_ref, sems):
    pair = (lax.axis_index("lat") + which) % 2
    copies = []
    for block in range(4):
        rows = pl.ds(block * (RINGS // 4), RINGS // 4)
        copies.append(
            pltpu.make_async_copy(table_ref.at[pair, rows, :], held_ref.at[rows, :], sems.at[block])
        )
    for copy in copies:
        copy.start()
    for copy in copies:
        copy.wait()


def gather_kernel(first_ref, second_ref, third_ref, fourth_ref, _, keep_ref, send_ref):
    total = (first_ref[...] + second_ref[...]) + (third_ref[...] + fourth_ref[...])
    keep_ref[...], send_ref[...] = total[:16], total[16:]


def halve_kernel(first_ref, second_ref, _, keep_ref, send_ref):
    total = first_ref[...] + second_ref[...]
    keep_ref[...], send_ref[...] = total[:8], total[8:]


def table_kernel(orders_ref, after_ref, out_ref):
    row = lax.broadcasted_iota(jnp.int32, (ROWS, 1), 0)
    first = lax.axis_index("ord")
    orders = orders_ref[:, 0:1]
    fraction = orders.astype(jnp.float32) * (1.0 / LMAX)
    wave = cosine_of(orders, row % 2, first) * (1.0 / math.sqrt(BAND))
    turned = cosine_of(orders, row % 2 + 1, first) * (1.0 / math.sqrt(BAND))
    for index, table in enumerate((wave, fraction * turned, fraction * fraction * wave)):
        rounded = table.astype(jnp.bfloat16)
        out_ref[index, 0:ROWS, :] = rounded
        out_ref[index, ROWS:, :] = rounded


def analysis_kernel(which, first_ref, second_ref, info_ref, table_ref, out_ref):
    pair = (lax.axis_index("lat") + which) % 2
    first_len = LMAX + 1 - info_ref[2 + which : 3 + which, 0:1].astype(jnp.int32)
    total = first_ref[...] + second_ref[...]
    weighted = total * (info_ref[0:1, :] * (1.0 / math.sqrt(16 * RINGS)))
    mine = jnp.where(pair == 1, weighted[4:8], weighted[0:4])
    left, right = mine[:, :RINGS], mine[:, RINGS:]
    rows = jnp.concatenate([left[0:2], right[0:2], left[2:4], right[2:4]], axis=0).astype(
        jnp.bfloat16
    )
    step = 1536
    for start in range(0, PACK, step):
        size = min(step, PACK - start)
        product = jnp.dot(
            rows, table_ref[:, start : start + size], preferred_element_type=jnp.float32
        )
        position = start + lax.broadcasted_iota(jnp.int32, (4, size), 1)
        out_ref[:, start : start + size] = jnp.where(
            position >= first_len, product[4:8], product[0:4]
        )
    out_ref[:, PACK:] = jnp.zeros((4, PADDED - PACK), jnp.float32)


def turn_kernel(own_ref, other_ref, _, own_out_ref, other_out_ref):
    step = 1536
    for table_ref, out_ref in ((own_ref, own_out_ref), (other_ref, other_out_ref)):
        for start in range(0, WHOLE, step):
            out_ref[start : start + step, :] = table_ref[:, start : start + step].T
        rest = jnp.concatenate(
            [table_ref[:, WHOLE:], jnp.zeros((RINGS, PADDED - PACK), jnp.bfloat16)], axis=1
        )
        out_ref[WHOLE:, :] = rest.T


def add_kernel(first_ref, second_ref, *rest):
    out_ref = rest[-1]
    out_ref[...] = first_ref[...] + second_ref[...]


def factor_kernel(which, info_ref, _, out_ref):
    order = info_ref[2 + which : 3 + which, 0:1].astype(jnp.int32)
    row = lax.broadcasted_iota(jnp.int32, (8, 1), 0)
    upper = (row // 2) % 2 == 1
    first_len = LMAX + 1 - order
    base = jnp.where(upper, -1, order)
    own_order = jnp.where(upper, LMAX - order, order).astype(jnp.float32)
    length = jnp.where(upper, order + 1, first_len).astype(jnp.float32)
    begin = jnp.where(upper, first_len, 0)
    end = jnp.where(upper, PACK, first_len)
    scaling = 1.0 / jnp.sqrt(length)
    step = 1536
    for start in range(0, PADDED, step):
        size = min(step, PADDED - start)
        position = start + lax.broadcasted_iota(jnp.int32, (8, size), 1)
        inside = (position >= begin) & (position < end)
        degree = (base + position).astype(jnp.float32)
        plain = jnp.where(inside, scaling, 0.0)
        sloped = plain * (degree * (1.0 / LMAX))
        out_ref[0, :, start : start + size] = plain
        out_ref[1, :, start : start + size] = sloped
        out_ref[2, :, start : start + size] = jnp.where(
            inside & (position < end - 1),
            (degree + (1.0 + own_order)) * (scaling * (1.0 / LMAX)),
            0.0,
        )
        out_ref[3, :, start : start + size] = sloped * ((degree + 1.0) * (1.0 / LMAX))


def synthesis_kernel(which, coeffs_ref, info_ref, table_ref, factor_ref, *rest):
    step = 1536
    synth = jnp.zeros((32, RINGS), jnp.float32)
    for start in range(0, PADDED, step):
        size = min(step, PADDED - start)
        own = coeffs_ref[:, start : start + size]
        if start + size < PADDED:
            ahead = coeffs_ref[:, start + size : start + size + 128]
        else:
            ahead = jnp.zeros((4, 128), jnp.float32)
        wide = jnp.concatenate([own, ahead], axis=1)
        after = pltpu.roll(wide, size + 127, axis=1)[:, :size]
        own, after = [
            jnp.concatenate([a[0:2], a[0:2], a[2:4], a[2:4]], axis=0) for a in (own, after)
        ]
        weights = jnp.concatenate(
            [
                (after if index == 2 else own) * factor_ref[index, :, start : start + size]
                for index in range(4)
            ],
            axis=0,
        ).astype(jnp.bfloat16)
        synth = synth + jnp.dot(
            weights, table_ref[start : start + size, :], preferred_element_type=jnp.float32
        )
    sine, cosine = info_ref[0:1, :RINGS], info_ref[1:2, :RINGS]
    fields = [synth[0:8], (cosine * synth[8:16] - synth[16:24]) / sine, synth[24:32]]
    fields = [jnp.concatenate([a[0:4], a[4:8]], axis=1) for a in fields]
    if which == 0:
        (out_ref,) = rest
        for index in range(3):
            out_ref[4 * index : 4 * index + 4, :] = fields[index]
    else:
        other_ref, _, out_ref = rest
        for index in range(3):
            rows = jnp.concatenate([other_ref[4 * index : 4 * index + 4, :], fields[index]], axis=0)
            out_ref[8 * index : 8 * index + 8, :] = rows


def inverse_kernel(*refs):
    blocks, (info_ref, table_ref, steep_ref, bend_ref, left_ref) = refs[:4], refs[4:]

    @pl.when(pl.program_id(0) == 0)
    def _():
        inverse = (1.0 / info_ref[...]).T[:, 0:1]
        first, slope, laplace = [
            jnp.concatenate(
                [ref[:, 8 * index : 8 * index + 8, :].reshape(ROWS // 4, 2 * RINGS) for ref in blocks],
                axis=0,
            ).T
            for index in range(3)
        ]
        scaled = first * inverse
        half = (0.5 * scaled) * inverse
        for index, rows in enumerate((slope, 0.5 * laplace, scaled, slope * inverse, half)):
            high = rows.astype(jnp.bfloat16)
            low = (rows - high.astype(jnp.float32)).astype(jnp.bfloat16)
            for layer in range(2):
                here = slice(layer * RINGS, (layer + 1) * RINGS)
                there = slice(index * RINGS, (index + 1) * RINGS)
                left_ref[layer, there, 0:ROWS] = high[here]
                left_ref[layer, there, ROWS:] = low[here]

    for start in range(0, MERIDIANS, COLUMNS):
        here = slice(start, min(start + COLUMNS, MERIDIANS))

        def to_grids(first, count, table):
            rows = left_ref[pl.program_id(0), first * RINGS : (first + count) * RINGS, :]
            product = jnp.dot(rows, table_ref[table, :, here], preferred_element_type=jnp.float32)
            return [product[index * RINGS : (index + 1) * RINGS] for index in range(count)]

        p, half_l = to_grids(0, 2, 0)
        q, s = to_grids(2, 2, 1)
        (half_t,) = to_grids(4, 1, 2)
        p2, q2 = p * p, q * q
        outer = 1.0 + q2
        area = outer + p2
        root = lax.rsqrt(area)
        steep_ref[0, :, here] = (area * root).astype(jnp.bfloat16)
        top = (q2 - p2) * half_t - outer * half_l - (p * q) * s
        bend_ref[0, :, here] = (top * (root * root * root)).astype(jnp.bfloat16)


VMEM = pl.BlockSpec(memory_space=pltpu.VMEM)
SMEM = pl.BlockSpec(memory_space=pltpu.SMEM)


ANY = pl.BlockSpec(memory_space=pl.ANY)


COST = pl.CostEstimate(flops=1000000000, bytes_accessed=4000000, transcendentals=0)


def call(kernel, shape, dtype, in_specs, limit=24, **kwargs):
    return pl.pallas_call(
        kernel,
        out_shape=jax.ShapeDtypeStruct(shape, dtype),
        in_specs=in_specs,
        out_specs=VMEM,
        compiler_params=pltpu.CompilerParams(vmem_limit_bytes=limit << 20),
        **kwargs,
    )


def on_device(altitude_grids, polynomial_values, span_azimuthal_modes, slot_mapping):
    layers, rings, meridians = altitude_grids.shape
    n_ord = lax.axis_size("ord")
    lines = layers * rings

    def from_back(value, stride, step):
        size = 4 * stride
        return lax.ppermute(
            value, "ord", [(k, k // size * size + (k + stride * step) % size) for k in range(n_ord)]
        )

    small = jnp.stack([span_azimuthal_modes, slot_mapping])
    wave = call(prepare_kernel, (ROWS, meridians), jnp.bfloat16, [VMEM], cost_estimate=COST)(small)
    product = pl.pallas_call(
        forward_kernel,
        out_shape=[jax.ShapeDtypeStruct((32, lines), jnp.float32)] * 4,
        in_specs=[VMEM] * 2,
        out_specs=[VMEM] * 4,
        compiler_params=pltpu.CompilerParams(vmem_limit_bytes=24 << 20),
    )(wave, altitude_grids)
    info, orders = pl.pallas_call(
        info_kernel,
        out_shape=[
            jax.ShapeDtypeStruct((8, lines), jnp.float32),
            jax.ShapeDtypeStruct((ROWS, 128), jnp.int32),
        ],
        in_specs=[VMEM, ANY],
        out_specs=[VMEM] * 2,
        cost_estimate=COST,
        compiler_params=pltpu.CompilerParams(vmem_limit_bytes=24 << 20),
    )(small, product[0])
    parts = [product[0]] + [from_back(product[a], 1, STEPS[a]) for a in (1, 2, 3)]

    def hold(which, after):
        return call(
            functools.partial(hold_kernel, which),
            polynomial_values.shape[1:],
            jnp.bfloat16,
            [ANY, ANY],
            limit=44,
            cost_estimate=COST,
            scratch_shapes=[pltpu.SemaphoreType.DMA((4,))],
        )(polynomial_values, after)

    def summed(kernel, rows, values, after):
        return pl.pallas_call(
            kernel,
            out_shape=[jax.ShapeDtypeStruct((rows, lines), jnp.float32)] * 2,
            in_specs=[VMEM] * len(values) + [ANY],
            out_specs=[VMEM] * 2,
            compiler_params=pltpu.CompilerParams(vmem_limit_bytes=24 << 20),
        )(*values, after)

    other_table = hold(1, product[0])
    keep, send = summed(gather_kernel, 16, parts, other_table)
    own_table = hold(0, keep)
    keep, send = summed(halve_kernel, 8, [keep, swap(send, "ord", 4)], own_table)
    parts = [keep, swap(send, "ord", 12)]
    tables_held = (own_table, other_table)

    def analysis(which):
        return call(
            functools.partial(analysis_kernel, which), (4, PADDED), jnp.float32, [VMEM] * 4
        )(*parts, info, tables_held[which])

    outgoing = analysis(1)
    other = swap(outgoing, "lat", 1)
    coeffs = analysis(0) + other
    tables = call(table_kernel, (3, 2 * ROWS, meridians), jnp.bfloat16, [VMEM, ANY], cost_estimate=COST)(
        orders, outgoing
    )

    def exchanged(value, even, odd):
        n = lax.axis_size("lat")
        return lax.ppermute(value, "lat", [(k, k ^ (odd if k % 2 else even)) for k in range(n)])

    def summed_with(value, received, *done):
        return call(add_kernel, (4, PADDED), jnp.float32, [VMEM] * 2 + [ANY] * len(done))(
            value, received, *done
        )

    def factor(which, after):
        return call(
            functools.partial(factor_kernel, which),
            (4, 8, PADDED),
            jnp.float32,
            [VMEM, ANY],
            cost_estimate=COST,
        )(info, after)

    factors = [factor(which, coeffs) for which in (0, 1)]
    coeffs = summed_with(coeffs, exchanged(coeffs, 2, 6), *factors)
    coeffs = summed_with(coeffs, exchanged(coeffs, 6, 8), tables)
    own_turned, other_turned = pl.pallas_call(
        turn_kernel,
        out_shape=[jax.ShapeDtypeStruct((PADDED, rings), jnp.bfloat16)] * 2,
        in_specs=[VMEM, VMEM, ANY],
        out_specs=[VMEM] * 2,
        cost_estimate=COST,
        compiler_params=pltpu.CompilerParams(vmem_limit_bytes=24 << 20),
    )(own_table, other_table, coeffs)
    coeffs = summed_with(coeffs, exchanged(coeffs, 8, 2), own_turned, other_turned)
    other = swap(coeffs, "lat", 1)

    mine = call(
        functools.partial(synthesis_kernel, 0), (12, layers * rings), jnp.float32, [VMEM] * 4
    )(coeffs, info, own_turned, factors[0])
    fields = call(
        functools.partial(synthesis_kernel, 1),
        (24, layers * rings),
        jnp.float32,
        [VMEM] * 5 + [ANY],
    )(other, info, other_turned, factors[1], mine, tables)

    column = jnp.stack([fields] + [from_back(fields, 4, step) for step in STEPS[1:]])
    blocks = [column] + [from_back(column, 1, step) for step in STEPS[1:]]

    block = pl.BlockSpec((1, rings, meridians), lambda f: (f, 0, 0))
    return pl.pallas_call(
        inverse_kernel,
        grid=(layers,),
        out_shape=[jax.ShapeDtypeStruct((layers, rings, meridians), jnp.bfloat16)] * 2,
        in_specs=[VMEM] * 6,
        out_specs=[block, block],
        scratch_shapes=[pltpu.VMEM((layers, 5 * rings, 2 * ROWS), jnp.bfloat16)],
        compiler_params=pltpu.CompilerParams(vmem_limit_bytes=32 << 20),
    )(*blocks, info, tables)


def solution(mesh):
    return jax.shard_map(
        on_device,
        mesh=mesh,
        in_specs=(P(None, "lat", "ord"), P("ord", "lat", None), P(), P()),
        out_specs=(P(None, "lat", "ord"), P(None, "lat", "ord")),
        check_vma=False,
    )
```
